256 devices in a mesh: lat: 8 (over y_hi, x), lon: 32 (over z, y_lo, core).
Axes of the slice: x: 4, y: 4 (y_hi: 2, y_lo: 2; y = y_hi * 2 + y_lo), z: 8, core: 2. Of those that a mesh axis runs over, the one named last changes fastest.
Arguments:
- adj_height: float32 [3, 3, 128, 24576], P(None, None, 'lat', 'lon'), may hold values from -6 to 6
- adj_east: float32 [3, 3, 128, 24576], P(None, None, 'lat', 'lon'), may hold values from -6 to 6
- adj_north: float32 [3, 3, 128, 24576], P(None, None, 'lat', 'lon'), may hold values from -6 to 6
- flow_east: float32 [3, 3, 128, 24576], P(None, None, 'lat', 'lon'), may hold values from -6 to 6
- flow_north: float32 [3, 3, 128, 24576], P(None, None, 'lat', 'lon'), may hold values from -6 to 6
- depth: float32 [3, 3, 128, 24576], P(None, None, 'lat', 'lon'), may hold values from 0.5 to 2
- friction: float32 [128, 24576], P('lat', 'lon'), may hold values from 0.2 to 2
- wet_dry: int32 [128, 24576], P('lat', 'lon'), may hold values 0 or 1
- sea_mask: int32 [128, 24576], P('lat', 'lon'), may hold values 0 or 1
- grad_depth: float32 [3, 3, 128, 24576], P(None, None, 'lat', 'lon'), may hold values from -6 to 6
- grad_friction: float32 [128, 24576], P('lat', 'lon'), may hold values from -6 to 6
- gauss_index: int32 [2048, 4096], P('lat', 'lon'), may hold values from 0 to 110591, as said below
- legendre: bfloat16 [256, 2048, 2048], P('lon', None, 'lat'), may hold values from -0.125 to 0.125
- love_gain: float32 [2048], replicated, may hold values from 0.3 to 3
Outputs:
- new_height: float32 [3, 3, 128, 24576], P(None, None, 'lat', 'lon')
- new_east: float32 [3, 3, 128, 24576], P(None, None, 'lat', 'lon')
- new_north: float32 [3, 3, 128, 24576], P(None, None, 'lat', 'lon')
- depth_grad: float32 [3, 3, 128, 24576], P(None, None, 'lat', 'lon')
- friction_grad: float32 [128, 24576], P('lat', 'lon')
The draws below stay inside these ranges and needn't reach their ends.
Inputs may be any that keep to these rules, and one draw needn't show every extreme that they name: `gauss_index`: each entry names a node of the cells of the same tile, as its position among that tile's 9 * 16 * 768 nodes flattened in the order latitude node, longitude node, cell row, cell column. The node lies in cell row (the point's latitude within its tile) // ((2048 / 8) / 16) of the tile.
All inputs are finite; a program needn't handle non-finite values. No bound on the sum of `wet_dry` or of `sea_mask` on one device may be relied on, other than what follows from the above.
Results may differ from the reference program's by a relative error of at most 0.00085.
Values may be sent and summed in bfloat16 or wider, within the bound.
No kernel may reach another device: no remote copies, remote signals or barrier semaphores. Data moves between devices by JAX's collectives and lax.ppermute only.
A program may use at most 128 MiB of HBM per device.

```python
import math
import jax
import jax.numpy as jnp
from jax import lax

NLAT = 2048
NLON = 4096
DEG = 2048
CLAT = 16
CLON = 768
MODES = 256
NCLAT = 128
NCLON = 24576
N_LAT = 8
N_LON = 32


def draw_gauss_index(key, part):
    key = jax.random.fold_in(key, 11)
    tile_rows = NLAT // N_LAT
    tile_cols = NLON // N_LON
    per_row = tile_rows // CLAT
    key_class, key_column = jax.random.split(key)
    node_class = jax.random.randint(key_class, (NLAT, NLON), 0, 9, dtype=jnp.int32)
    column = jax.random.randint(key_column, (NLAT, NLON), 0, CLON, dtype=jnp.int32)
    local_row = jnp.arange(NLAT, dtype=jnp.int32) % tile_rows
    local_col = jnp.arange(NLON, dtype=jnp.int32) % tile_cols
    row_cells = local_row // per_row
    result = node_class * (CLAT * CLON) + row_cells[:, None] * CLON + column
    first_point = (local_row[:, None] == 0) & (local_col[None, :] == 0)
    last_point = (local_row[:, None] == tile_rows - 1) & (local_col[None, :] == tile_cols - 1)
    result = jnp.where(first_point, 0, result)
    result = jnp.where(last_point, 9 * CLAT * CLON - 1, result)
    return result.astype(jnp.int32)


def set_ends(values, rng, least, top_value):
    spot = [jax.random.randint(jax.random.fold_in(rng, axis), (), 0, length) for axis, length in enumerate(values.shape)]
    main_axis = values.shape.index(max(values.shape))
    next_to = spot[:main_axis] + [(spot[main_axis] + 1) % values.shape[main_axis]] + spot[main_axis + 1:]
    return values.at[tuple(spot)].set(least).at[tuple(next_to)].set(top_value)


def block_scale(stream_key, dims, shards, low, high):
    level, own = 1.0, jax.random.fold_in(stream_key, 6)
    for axis_at, parts in shards:
        draws = jnp.exp(jax.random.uniform(jax.random.fold_in(own, axis_at), (parts,), jnp.float32, low / len(shards), high / len(shards)))
        level = level * jnp.repeat(draws, dims[axis_at] // parts).reshape([-1 if axis == axis_at else 1 for axis in range(len(dims))])
    return level


def gaussian(rng, dims, spread, bound, shards=(), kind=jnp.bfloat16):
    level = block_scale(rng, dims, shards, -0.22, 0.18) if shards else 1.0
    array = jax.random.normal(rng, dims, jnp.float32) * spread * level
    return jnp.minimum(jnp.maximum(array, -bound), bound).astype(kind)


def setup_inputs(seed: int = 0) -> dict:
    key_list = jax.random.split(jax.random.key(seed), 15)
    return {
        "adj_height": gaussian(key_list[0], (3, 3, NCLAT, NCLON), 1.0, 6.0, ((2, 8), (3, 32)), jnp.float32),
        "adj_east": gaussian(key_list[1], (3, 3, NCLAT, NCLON), 1.0, 6.0, ((2, 8), (3, 32)), jnp.float32),
        "adj_north": gaussian(key_list[2], (3, 3, NCLAT, NCLON), 1.0, 6.0, ((2, 8), (3, 32)), jnp.float32),
        "flow_east": gaussian(key_list[3], (3, 3, NCLAT, NCLON), 1.0, 6.0, ((2, 8), (3, 32)), jnp.float32),
        "flow_north": gaussian(key_list[4], (3, 3, NCLAT, NCLON), 1.0, 6.0, ((2, 8), (3, 32)), jnp.float32),
        "depth": jnp.clip(jnp.exp(math.log(2.0) - 1.3862944 * jax.random.uniform(key_list[5], (3, 3, NCLAT, NCLON), jnp.float32) ** block_scale(key_list[5], (3, 3, NCLAT, NCLON), ((2, 8), (3, 32)), -0.2, 0.2)), 0.5, 2.0),
        "friction": jnp.clip(jnp.exp(math.log(2.0) - 2.3025851 * jax.random.uniform(key_list[6], (NCLAT, NCLON), jnp.float32) ** block_scale(key_list[6], (NCLAT, NCLON), ((0, 8), (1, 32)), -0.2, 0.2)), 0.2, 2.0),
        "wet_dry": set_ends((jax.random.randint(key_list[7], (NCLAT, NCLON), 0, 8) < 7).astype(jnp.int32), jax.random.fold_in(key_list[7], 1), 0, 1),
        "sea_mask": set_ends((jax.random.randint(key_list[8], (NCLAT, NCLON), 0, 5) < 4).astype(jnp.int32), jax.random.fold_in(key_list[8], 1), 0, 1),
        "grad_depth": gaussian(key_list[9], (3, 3, NCLAT, NCLON), 1.0, 6.0, ((2, 8), (3, 32)), jnp.float32),
        "grad_friction": gaussian(key_list[10], (NCLAT, NCLON), 1.0, 6.0, ((0, 8), (1, 32)), jnp.float32),
        "gauss_index": draw_gauss_index(jax.random.fold_in(key_list[14], 71), 0),
        "legendre": gaussian(key_list[12], (MODES, DEG, NLAT), NLAT ** -0.5, 0.125, ((0, 32), (2, 8))),
        "love_gain": jnp.clip(jnp.exp(jax.random.uniform(key_list[13], (DEG,), jnp.float32, math.log(0.3), math.log(3.0))), 0.3, 3.0),
    }


stencil = ((-1.5, 2.0, -0.5), (-0.5, 0.0, 0.5), (0.5, -2.0, 1.5))
penalty = 1.5
courant = 0.3

def inner_part(layers):
    return [stencil[target][0] * layers[0] + stencil[target][1] * layers[1] + stencil[target][2] * layers[2] for target in range(3)]

def along_lon(field):
    layers = [field[:, column] for column in range(3)]
    previous = jnp.roll(layers[2], 1, axis=2)
    following = jnp.roll(layers[0], -1, axis=2)
    result = inner_part(layers)
    result[0] = result[0] + penalty * (layers[0] - previous)
    result[2] = result[2] + penalty * (following - layers[2])
    return jnp.stack(result, axis=1)

def along_lat(field):
    layers = [field[column] for column in range(3)]
    border = jnp.zeros_like(layers[0][:, :1, :])
    previous = jnp.concatenate([border, layers[2][:, :-1, :]], axis=1)
    following = jnp.concatenate([layers[0][:, 1:, :], border], axis=1)
    result = inner_part(layers)
    result[0] = result[0] + penalty * (layers[0] - previous)
    result[2] = result[2] + penalty * (following - layers[2])
    return jnp.stack(result, axis=0)

def transposed(operator, cotangent):
    _, pullback = jax.vjp(operator, cotangent)
    return pullback(cotangent)[0]

def grid_tiles(grid_field, tile_rows, tile_cols):
    return grid_field.reshape(N_LAT, tile_rows, N_LON, tile_cols).transpose(0, 2, 1, 3).reshape(N_LAT * N_LON, tile_rows * tile_cols)

def loading(source, gauss_index, legendre, love_gain):
    node_count = 9 * CLAT * CLON
    tile_rows = NLAT // N_LAT
    tile_cols = NLON // N_LON
    node_tiles = source.reshape(3, 3, N_LAT, CLAT, N_LON, CLON).transpose(2, 4, 0, 1, 3, 5).reshape(N_LAT * N_LON, node_count)
    index_tiles = grid_tiles(gauss_index, tile_rows, tile_cols)
    sampled_tiles = jnp.take_along_axis(node_tiles, index_tiles, axis=1)
    sampled = sampled_tiles.reshape(N_LAT, N_LON, tile_rows, tile_cols).transpose(0, 2, 1, 3).reshape(NLAT, NLON)
    wave_numbers = jnp.arange(MODES, dtype=jnp.int32)
    places = jnp.arange(NLON, dtype=jnp.int32)
    phase_index = wave_numbers[:, None] * places[None, :] % NLON
    angle_table = phase_index.astype(jnp.float32) * (2.0 * math.pi / NLON)
    cosine_table = jnp.cos(angle_table)
    sine_table = jnp.sin(angle_table)
    norm_factor = math.sqrt(2.0 / NLON)
    real_part = norm_factor * jnp.dot(cosine_table, sampled.T, precision=lax.Precision.HIGHEST, preferred_element_type=jnp.float32)
    imag_part = -norm_factor * jnp.dot(sine_table, sampled.T, precision=lax.Precision.HIGHEST, preferred_element_type=jnp.float32)
    spectrum = jnp.stack((real_part, imag_part), axis=1).astype(jnp.bfloat16)
    degrees = jnp.arange(DEG, dtype=jnp.int32)

    def per_mode(inputs):
        mode_spectrum, mode_table, wave_number = inputs
        table_wide = mode_table.astype(jnp.float32)
        coeffs = jnp.dot(mode_spectrum.astype(jnp.float32), table_wide.T, precision=lax.Precision.HIGHEST, preferred_element_type=jnp.float32)
        live_mask = (degrees >= wave_number).astype(jnp.float32)
        scaled = (coeffs * (love_gain * live_mask)[None, :]).astype(jnp.bfloat16)
        return jnp.dot(scaled.astype(jnp.float32), table_wide, precision=lax.Precision.HIGHEST, preferred_element_type=jnp.float32)
    synthesis = lax.map(per_mode, (spectrum, legendre, wave_numbers))
    grid_field = norm_factor * (jnp.dot(synthesis[:, 0, :].T, cosine_table, precision=lax.Precision.HIGHEST, preferred_element_type=jnp.float32) - jnp.dot(synthesis[:, 1, :].T, sine_table, precision=lax.Precision.HIGHEST, preferred_element_type=jnp.float32))
    field_tiles = grid_tiles(grid_field, tile_rows, tile_cols)
    offsets = jnp.arange(N_LAT * N_LON, dtype=jnp.int32)[:, None] * node_count + index_tiles
    summed = jax.ops.segment_sum(field_tiles.reshape(-1), offsets.reshape(-1), num_segments=N_LAT * N_LON * node_count)
    return summed.reshape(N_LAT, N_LON, 3, 3, CLAT, CLON).transpose(2, 3, 0, 4, 1, 5).reshape(3, 3, NCLAT, NCLON)

def reference(adj_height, adj_east, adj_north, flow_east, flow_north, depth, friction, wet_dry, sea_mask, grad_depth, grad_friction, gauss_index, legendre, love_gain):
    wet_cells = (wet_dry * sea_mask).astype(jnp.float32)
    lon_east = transposed(along_lon, wet_cells * adj_east)
    lat_north = transposed(along_lat, wet_cells * adj_north)
    lon_height = transposed(along_lon, wet_cells * adj_height)
    lat_height = transposed(along_lat, wet_cells * adj_height)
    source = lon_east + lat_north
    loaded = loading(source, gauss_index, legendre, love_gain)
    new_height = adj_height - courant * (source - loaded)
    retain = wet_cells * (1.0 - courant * friction)
    new_east = retain * adj_east - courant * depth * wet_cells * lon_height
    new_north = retain * adj_north - courant * depth * wet_cells * lat_height
    depth_grad = grad_depth - courant * wet_cells * (flow_east * lon_height + flow_north * lat_height)
    friction_grad = grad_friction - courant * wet_cells * lax.optimization_barrier(jnp.sum(flow_east * adj_east + flow_north * adj_north, axis=(0, 1)))
    return (new_height, new_east, new_north, depth_grad, friction_grad)
```

```python
import functools
import math

import jax
import jax.numpy as jnp
from jax import lax
from jax.experimental import pallas as pl
from jax.experimental.pallas import tpu as pltpu
from jax.sharding import PartitionSpec as P

courant = 0.3
lanes = 128


def neighbours(axis, periodic):
    count = lax.axis_size(axis)
    forward = [(i, i + 1) for i in range(count - 1)]
    if periodic:
        forward.append((count - 1, 0))
    return forward, [(target, source) for source, target in forward]


def wave_pair(phase, circle):
    quarter = circle // 4
    turn = lax.shift_right_arithmetic(phase + quarter // 2, int(math.log2(quarter)))
    angle = (phase - turn * quarter).astype(jnp.float32) * (2.0 * math.pi / circle)
    square = angle * angle
    sine = angle * (
        1.0
        + square * (-1.0 / 6 + square * (1.0 / 120 + square * (-1.0 / 5040 + square / 362880)))
    )
    cosine = 1.0 + square * (
        -0.5 + square * (1.0 / 24 + square * (-1.0 / 720 + square / 40320))
    )
    odd = (turn & 1) == 1
    cos_out = jnp.where(odd, sine, cosine)
    sin_out = jnp.where(odd, cosine, sine)
    cos_out = jnp.where(((turn + 1) & 2) == 2, -cos_out, cos_out)
    sin_out = jnp.where((turn & 2) == 2, -sin_out, sin_out)
    return cos_out, sin_out


def wave_table(sector, sectors, mode_local, grid_cols):
    circle = sectors * grid_cols
    modes = sectors * mode_local
    wave = lax.broadcasted_iota(jnp.int32, (modes, grid_cols), 0)
    place = lax.broadcasted_iota(jnp.int32, (modes, grid_cols), 1) + sector * grid_cols
    cosine, sine = wave_pair(wave * place, circle)
    norm = math.sqrt(2.0 / circle)
    table = jnp.stack(
        (
            (norm * cosine).reshape(sectors, mode_local, grid_cols),
            (-norm * sine).reshape(sectors, mode_local, grid_cols),
        ),
        axis=1,
    )
    return table.reshape(2 * modes, grid_cols)


def two_parts(value):
    high = value.astype(jnp.bfloat16)
    return high, (value - high.astype(jnp.float32)).astype(jnp.bfloat16)


def contract(left, right, dims):
    return lax.dot_general(left, right, (dims, ((), ())), preferred_element_type=jnp.float32)


def contract_split(left, right, dims):
    left_high, left_low = two_parts(left)
    right_high, right_low = two_parts(right)
    return (
        contract(left_high, right_high, dims)
        + contract(left_high, right_low, dims)
        + contract(left_low, right_high, dims)
    )


def as_column(row):
    count = row.shape[1]
    grid = jnp.broadcast_to(row, (count, count))
    diagonal = lax.broadcasted_iota(jnp.int32, (count, count), 0) == lax.broadcasted_iota(
        jnp.int32, (count, count), 1
    )
    return jnp.sum(jnp.where(diagonal, grid, 0.0), axis=1, keepdims=True)


def lon_lines(first, middle, last, west, east):
    columns = first.shape[1]
    place = lax.broadcasted_iota(jnp.int32, first.shape, 1)
    previous = jnp.where(place == 0, as_column(west), pltpu.roll(last, 1, 1))
    following = jnp.where(place == columns - 1, as_column(east), pltpu.roll(first, columns - 1, 1))
    return (
        0.5 * (last - middle) + 1.5 * previous,
        2.0 * (first - last),
        0.5 * (middle - first) - 1.5 * following,
    )


def lat_lines(first, middle, last, north, south):
    rows = first.shape[0]
    place = lax.broadcasted_iota(jnp.int32, first.shape, 0)
    previous = jnp.where(place == 0, north, pltpu.roll(last, 1, 0))
    following = jnp.where(place == rows - 1, south, pltpu.roll(first, rows - 1, 0))
    return (
        0.5 * (last - middle) + 1.5 * previous,
        2.0 * (first - last),
        0.5 * (middle - first) - 1.5 * following,
    )


def wet_of(wet_ref, sea_ref):
    return (wet_ref[...] * sea_ref[...]).astype(jnp.float32)


def source_kernel(
    sectors,
    mode_local,
    east_ref,
    north_ref,
    wet_ref,
    sea_ref,
    west_halo,
    east_halo,
    north_halo,
    south_halo,
    index_ref,
    source_ref,
    partial_ref,
    sampled_ref,
):
    wet = wet_of(wet_ref, sea_ref)
    cell_rows, cell_cols = wet.shape
    chunks = cell_cols // lanes
    for a in range(3):
        lines = lon_lines(
            *(wet * east_ref[a, b] for b in range(3)),
            west_halo[0, a : a + 1, :],
            east_halo[0, a : a + 1, :],
        )
        for b in range(3):
            for t in range(chunks):
                source_ref[(3 * a + b) * chunks + t] = lines[b][:, t * lanes : (t + 1) * lanes]
    for b in range(3):
        lines = lat_lines(
            *(wet * north_ref[a, b] for a in range(3)),
            north_halo[0, b : b + 1, :],
            south_halo[0, b : b + 1, :],
        )
        for a in range(3):
            for t in range(chunks):
                source_ref[(3 * a + b) * chunks + t] += lines[a][:, t * lanes : (t + 1) * lanes]

    grid_rows, grid_cols = index_ref.shape
    per_row = grid_rows // cell_rows
    stride = cell_rows * cell_cols // lanes

    def sample_row(row, carry):
        points = pl.ds(pl.multiple_of(row * per_row, per_row), per_row)
        place = index_ref[points, :] - row * cell_cols
        chunk = lax.shift_right_arithmetic(place, 7)
        lane = place & (lanes - 1)
        total = jnp.zeros(place.shape, jnp.float32)
        for node in range(9):
            for t in range(chunks):
                line = source_ref[node * chunks + t, pl.ds(row, 1), :]
                picked = jnp.take_along_axis(
                    jnp.broadcast_to(line, (per_row, lanes)), lane, axis=1
                )
                total = jnp.where(chunk == node * stride + t, picked, total)
        sampled_ref[points, :] = total
        return carry

    lax.fori_loop(0, cell_rows, sample_row, 0)
    table = wave_table(lax.axis_index("lon"), sectors, mode_local, grid_cols)
    partial_ref[...] = contract_split(table, sampled_ref[...], ((1,), (1,))).reshape(
        partial_ref.shape
    )


def only_mode(values, mode, mode_local):
    row = lax.broadcasted_iota(jnp.int32, values.shape, 0)
    return jnp.where(lax.rem(row, mode_local) == mode, values, 0.0).astype(jnp.bfloat16)


def analysis_kernel(spectrum_ref, legendre_ref, coeffs_ref):
    mode_local = legendre_ref.shape[0]
    spectrum = spectrum_ref[...].astype(jnp.bfloat16).astype(jnp.float32)
    degrees = legendre_ref.shape[1]
    step = 512
    for start in range(0, degrees, step):
        total = None
        for mode in range(mode_local):
            term = contract(
                only_mode(spectrum, mode, mode_local),
                legendre_ref[mode, start : start + step, :],
                ((1,), (1,)),
            )
            total = term if total is None else total + term
        coeffs_ref[:, start : start + step] = total


def synthesis_kernel(coeffs_ref, gain_ref, legendre_ref, synthesis_ref):
    mode_local = legendre_ref.shape[0]
    coeffs = coeffs_ref[...]
    wave = lax.rem(lax.broadcasted_iota(jnp.int32, coeffs.shape, 0), mode_local)
    wave = wave + lax.axis_index("lon") * mode_local
    degree = lax.broadcasted_iota(jnp.int32, coeffs.shape, 1)
    scaled = jnp.where(degree >= wave, coeffs * gain_ref[...], 0.0)
    total = None
    for mode in range(mode_local):
        term = contract(
            only_mode(scaled, mode, mode_local), legendre_ref[mode], ((1,), (0,))
        )
        total = term if total is None else total + term
    synthesis_ref[...] = total


def height_kernel(
    sectors,
    mode_local,
    pieces_ref,
    index_ref,
    height_ref,
    source_ref,
    out_ref,
    field_ref,
    left_ref,
    right_ref,
    sums_ref,
):
    grid_rows, grid_cols = index_ref.shape
    cell_rows, cell_cols = height_ref.shape[2:]
    per_row = grid_rows // cell_rows
    chunks = cell_cols // lanes
    stride = cell_rows * cell_cols // lanes
    table = wave_table(lax.axis_index("lon"), sectors, mode_local, grid_cols)
    pieces = pieces_ref[...].reshape(2 * sectors * mode_local, grid_rows)
    field_ref[...] = contract_split(pieces, table, ((0,), (0,)))
    slots = left_ref.shape[0]
    slot = lax.broadcasted_iota(jnp.int32, (slots, lanes), 0)
    code = jnp.where(slot < 9 * chunks, slot // chunks * stride + slot % chunks, -1)
    lane_code = lax.broadcasted_iota(jnp.int32, (lanes, lanes), 0)

    def add_row(row, carry):
        for g in range(per_row):
            spot = row * per_row + g
            place = index_ref[pl.ds(spot, 1), :] - row * cell_cols
            chunk = lax.shift_right_arithmetic(place, 7)
            lane = place & (lanes - 1)
            value = field_ref[pl.ds(spot, 1), :]
            high = value.astype(jnp.bfloat16).astype(jnp.float32)
            low = value - high
            here = slice(g * lanes, (g + 1) * lanes)
            left_ref[:, here] = jnp.where(chunk == code, 1.0, 0.0).astype(jnp.bfloat16)
            match = lane == lane_code
            right_ref[:lanes, here] = jnp.where(match, high, 0.0).astype(jnp.bfloat16)
            right_ref[lanes:, here] = jnp.where(match, low, 0.0).astype(jnp.bfloat16)
        both = contract(left_ref[...], right_ref[...], ((1,), (1,)))
        sums_ref[row] = both[:, :lanes] + both[:, lanes:]
        return carry

    lax.fori_loop(0, cell_rows, add_row, 0)
    for node in range(9):
        for t in range(chunks):
            here = slice(t * lanes, (t + 1) * lanes)
            loaded = sums_ref[:, node * chunks + t, :]
            out_ref[node // 3, node % 3, :, here] = height_ref[
                node // 3, node % 3, :, here
            ] - courant * (source_ref[node * chunks + t] - loaded)


def flow_kernel(
    height_ref,
    east_ref,
    north_ref,
    flow_east_ref,
    flow_north_ref,
    depth_ref,
    friction_ref,
    wet_ref,
    sea_ref,
    grad_depth_ref,
    grad_friction_ref,
    west_halo,
    east_halo,
    north_halo,
    south_halo,
    new_east_ref,
    new_north_ref,
    depth_grad_ref,
    friction_grad_ref,
):
    wet = wet_of(wet_ref, sea_ref)
    retain = wet * (1.0 - courant * friction_ref[...])
    drag = jnp.zeros_like(wet)
    for a in range(3):
        lines = lon_lines(
            *(wet * height_ref[a, b] for b in range(3)),
            west_halo[1, a : a + 1, :],
            east_halo[1, a : a + 1, :],
        )
        for b in range(3):
            east = east_ref[a, b]
            flow = flow_east_ref[a, b]
            new_east_ref[a, b] = retain * east - courant * depth_ref[a, b] * wet * lines[b]
            depth_grad_ref[a, b] = grad_depth_ref[a, b] - courant * wet * (flow * lines[b])
            drag = drag + flow * east
    for b in range(3):
        lines = lat_lines(
            *(wet * height_ref[a, b] for a in range(3)),
            north_halo[1, b : b + 1, :],
            south_halo[1, b : b + 1, :],
        )
        for a in range(3):
            north = north_ref[a, b]
            flow = flow_north_ref[a, b]
            new_north_ref[a, b] = retain * north - courant * depth_ref[a, b] * wet * lines[a]
            depth_grad_ref[a, b] -= courant * wet * (flow * lines[a])
            drag = drag + flow * north
    friction_grad_ref[...] = grad_friction_ref[...] - courant * wet * drag


def shaped(shape, dtype=jnp.float32):
    return jax.ShapeDtypeStruct(shape, dtype)


def cost(flops, bytes_accessed):
    return pl.CostEstimate(flops=flops, bytes_accessed=bytes_accessed, transcendentals=0)


def params(mebibytes):
    return pltpu.CompilerParams(vmem_limit_bytes=mebibytes << 20)


def local(
    adj_height,
    adj_east,
    adj_north,
    flow_east,
    flow_north,
    depth,
    friction,
    wet_dry,
    sea_mask,
    grad_depth,
    grad_friction,
    gauss_index,
    legendre,
    love_gain,
):
    sectors = lax.axis_size("lon")
    mode_local, degrees, grid_rows = legendre.shape
    grid_cols = gauss_index.shape[1]
    cell_rows, cell_cols = wet_dry.shape
    nodes = adj_height.shape

    wet = (wet_dry * sea_mask).astype(jnp.float32)
    forward, backward = neighbours("lon", True)
    east_height = (adj_east, adj_height)
    west_halo = lax.ppermute(
        jnp.stack([wet[:, -1] * field[:, 2, :, -1] for field in east_height]), "lon", forward
    )
    east_halo = lax.ppermute(
        jnp.stack([wet[:, 0] * field[:, 0, :, 0] for field in east_height]), "lon", backward
    )
    forward, backward = neighbours("lat", False)
    north_height = (adj_north, adj_height)
    north_halo = lax.ppermute(
        jnp.stack([wet[-1] * field[2, :, -1, :] for field in north_height]), "lat", forward
    )
    south_halo = lax.ppermute(
        jnp.stack([wet[0] * field[0, :, 0, :] for field in north_height]), "lat", backward
    )
    halos = (west_halo, east_halo, north_halo, south_halo)

    source, partial = pl.pallas_call(
        functools.partial(source_kernel, sectors, mode_local),
        out_shape=(
            shaped((9 * cell_cols // lanes, cell_rows, lanes)),
            shaped((sectors, 2 * mode_local, grid_rows)),
        ),
        scratch_shapes=[pltpu.VMEM((grid_rows, grid_cols), jnp.float32)],
        cost_estimate=cost(200_000_000, 3_000_000),
        compiler_params=params(24),
        name="source_sampled",
    )(adj_east, adj_north, wet_dry, sea_mask, *halos, gauss_index)

    spectrum = lax.psum_scatter(partial, "lon", scatter_dimension=0, tiled=True)
    spectrum = spectrum.reshape(2 * mode_local, grid_rows)

    new_east, new_north, depth_grad, friction_grad = pl.pallas_call(
        flow_kernel,
        out_shape=(shaped(nodes), shaped(nodes), shaped(nodes), shaped(wet.shape)),
        cost_estimate=cost(20_000_000, 5_000_000),
        compiler_params=params(24),
        name="flow_terms",
    )(
        adj_height,
        adj_east,
        adj_north,
        flow_east,
        flow_north,
        depth,
        friction,
        wet_dry,
        sea_mask,
        grad_depth,
        grad_friction,
        *halos,
    )

    coeffs = pl.pallas_call(
        analysis_kernel,
        out_shape=shaped((2 * mode_local, degrees)),
        cost_estimate=cost(200_000_000, 8_000_000),
        compiler_params=params(24),
        name="legendre_analysis",
    )(spectrum, legendre)
    coeffs = lax.psum(coeffs, "lat")
    synthesis = pl.pallas_call(
        synthesis_kernel,
        out_shape=shaped((2 * mode_local, grid_rows)),
        cost_estimate=cost(200_000_000, 8_000_000),
        compiler_params=params(24),
        name="legendre_synthesis",
    )(coeffs, love_gain.reshape(1, degrees), legendre)
    pieces = lax.all_gather(synthesis, "lon", axis=0, tiled=False)
    slots = 9 * cell_cols // lanes + 10
    points = grid_rows // cell_rows * lanes
    new_height = pl.pallas_call(
        functools.partial(height_kernel, sectors, mode_local),
        out_shape=shaped(nodes),
        scratch_shapes=[
            pltpu.VMEM((grid_rows, grid_cols), jnp.float32),
            pltpu.VMEM((slots, points), jnp.bfloat16),
            pltpu.VMEM((2 * lanes, points), jnp.bfloat16),
            pltpu.VMEM((cell_rows, slots, lanes), jnp.float32),
        ],
        cost_estimate=cost(200_000_000, 3_000_000),
        compiler_params=params(24),
        name="height_loaded",
    )(pieces, gauss_index, adj_height, source)
    return (new_height, new_east, new_north, depth_grad, friction_grad)


def solution(mesh):
    field = P(None, None, "lat", "lon")
    cell = P("lat", "lon")
    in_specs = (
        field,
        field,
        field,
        field,
        field,
        field,
        cell,
        cell,
        cell,
        field,
        cell,
        cell,
        P("lon", None, "lat"),
        P(),
    )
    out_specs = (field, field, field, field, cell)
    return jax.shard_map(local, mesh=mesh, in_specs=in_specs, out_specs=out_specs, check_vma=False)
```
